32 devices in a mesh: groups: 2 (over y), expert: 4 (over z), tensor: 4 (over x, core).
Axes of the slice: x: 2, y: 2, z: 4, core: 2. Of those that a mesh axis runs over, the one named last changes fastest.
Arguments:
- partials: bfloat16 [4, 512, 7168], P('tensor', ('groups', 'expert')), parts along dimension 1, may hold values from -6 to 6
- norm_gain: float32 [7168], replicated, may hold values from 0.1 to 1.9
- expert_ids: int32 [512, 8], P(('groups', 'expert')), parts along dimension 0, may hold values from 0 to 255, as said below
- gate_values: float32 [512, 8], P(('groups', 'expert')), parts along dimension 0, may hold values from 0.1 to 1
- up_weight: bfloat16 [4, 7168, 512], P('expert', None, 'tensor'), may hold values from -0.0625 to 0.0625
- down_weight: bfloat16 [4, 512, 7168], P('expert', 'tensor'), may hold values from -0.25 to 0.25
Outputs:
- routed: bfloat16 [512, 7168], P(('groups', 'expert', 'tensor')), parts along dimension 0
The draws below stay inside these ranges and needn't reach their ends.
There are 2 independent parts, one for each index of `groups`. The reference program is written for one: setup_inputs(seed, part) draws one part's arguments, and reference() takes and returns one part's arrays. A program takes and returns all parts, laid end to end along the dimension named above; an argument that names none is the same for every part. Nothing has to cross between parts.
Inputs may be any that keep to these rules, and one draw needn't show every extreme that they name: `expert_ids`: each row names 8 different experts; only experts below 4 belong to the window. In each aligned block of 64 rows (one index of expert), a quarter of the window's experts are named exactly 4 times, a quarter 4 // 2 times and half 4 // 4 times; the quarter named 4 times is the same in every block.
All inputs are finite; a program needn't handle non-finite values.
Results may differ from the reference program's by a relative error of at most 0.018.
Values may be sent and summed in bfloat16 or wider, within the bound.
A program may use at most 64 MiB of HBM per device.

```python
import math
import jax
import jax.numpy as jnp
from jax import lax

MODEL_WIDTH = 7168
EXPERTS = 256
TOPK = 8
FF_DEV = 128
CAP = 4
TOK_DEV = 16
EXPERT_HIDDEN = 512
WINDOW_EXPERTS = 4
TOKENS = 256
N_EXPERT = 4
N_TENSOR = 4


def draw_expert_ids(key, part):
    key = jax.random.fold_in(key, 11)
    key_heavy, key_blocks = jax.random.split(key)
    rows_per_block = N_TENSOR * TOK_DEV
    owners = N_EXPERT
    quarter = owners // 4
    total = quarter * CAP + quarter * (CAP // 2) + (owners - 2 * quarter) * (CAP // 4)
    heavy_order = jax.random.permutation(key_heavy, owners)
    base_rank = jnp.argsort(heavy_order).astype(jnp.int32)

    def one_block(block_key):
        key_light, key_far, key_rows, key_slots = jax.random.split(block_key, 4)
        light = jax.random.permutation(key_light, owners - quarter)
        shifted = jnp.clip(base_rank - quarter, 0, owners - quarter - 1)
        rank_now = jnp.where(base_rank < quarter, base_rank, quarter + light[shifted])
        counts = jnp.where(rank_now < quarter, CAP, jnp.where(rank_now < 2 * quarter, CAP // 2, CAP // 4))
        ends = jnp.cumsum(counts)
        position = jnp.arange(TOPK * rows_per_block, dtype=jnp.int32)
        owner_at = jnp.sum((position[:, None] >= ends[None, :]).astype(jnp.int32), axis=1)
        far_start = jax.random.randint(key_far, (rows_per_block,), 0, EXPERTS - owners)
        slot_k = position // rows_per_block
        token_i = position % rows_per_block
        far_id = owners + (far_start[token_i] + slot_k) % (EXPERTS - owners)
        table_flat = jnp.where(position < total, owner_at, far_id)
        table = table_flat.reshape(TOPK, rows_per_block).T
        table = table[jax.random.permutation(key_rows, rows_per_block)]
        scores = jax.random.randint(key_slots, (rows_per_block, TOPK), 0, 1 << 20) * TOPK + jnp.arange(TOPK)[None, :]
        order = jnp.argsort(scores, axis=1)
        return jnp.take_along_axis(table, order, axis=1)
    blocks = jax.vmap(one_block)(jax.random.split(key_blocks, owners))
    return blocks.reshape(owners * rows_per_block, TOPK).astype(jnp.int32)


def block_levels(own_key, shape, cuts, smallest, top_value):
    factor_of, own = 1.0, jax.random.fold_in(own_key, 6)
    for dim, blocks in cuts:
        steps = jnp.exp(jax.random.uniform(jax.random.fold_in(own, dim), (blocks,), jnp.float32, smallest / len(cuts), top_value / len(cuts)))
        factor_of = factor_of * jnp.repeat(steps, shape[dim] // blocks).reshape([-1 if axis == dim else 1 for axis in range(len(shape))])
    return factor_of


def bell_draw(key, shape, deviation, bound, cuts=(), kind=jnp.bfloat16):
    gain = block_levels(key, shape, cuts, -0.22, 0.18) if cuts else 1.0
    drawn = jax.random.normal(key, shape, jnp.float32) * deviation * gain
    return jnp.minimum(jnp.maximum(drawn, -bound), bound).astype(kind)


def setup_inputs(seed: int = 0, part: int = 0) -> dict:
    keys = jax.random.split(jax.random.key(seed), 7)
    part_keys = jax.random.split(jax.random.fold_in(keys[6], part), 7)
    return {
        "partials": bell_draw(part_keys[0], (N_TENSOR, TOKENS, MODEL_WIDTH), 1.0, 6.0, ((0, 4), (1, 4))),
        "norm_gain": jnp.clip(1.0 + 0.18 * jax.random.normal(keys[1], (MODEL_WIDTH,), jnp.float32), 0.1, 1.9),
        "expert_ids": draw_expert_ids(jax.random.fold_in(jax.random.fold_in(keys[6], part), 71), part),
        "gate_values": jnp.clip(jnp.exp(math.log(1.0) - 2.3025851 * jax.random.uniform(part_keys[3], (TOKENS, TOPK), jnp.float32) ** block_levels(part_keys[3], (TOKENS, TOPK), ((0, 4),), -0.2, 0.2)), 0.1, 1.0),
        "up_weight": bell_draw(keys[4], (WINDOW_EXPERTS, MODEL_WIDTH, EXPERT_HIDDEN), MODEL_WIDTH ** -0.5, 0.0625, ((0, 4), (2, 4))),
        "down_weight": bell_draw(keys[5], (WINDOW_EXPERTS, EXPERT_HIDDEN, MODEL_WIDTH), EXPERT_HIDDEN ** -0.5, 0.25, ((0, 4), (1, 4))),
    }


def rms_norm(values, norm_gain):
    wide = values.astype(jnp.float32)
    mean_sq = lax.optimization_barrier(jnp.mean(wide * wide, axis=-1, keepdims=True))
    return (wide * lax.rsqrt(mean_sq + 1e-06) * norm_gain).astype(jnp.bfloat16)

def reference(partials, norm_gain, expert_ids, gate_values, up_weight, down_weight):
    attended = lax.optimization_barrier(jnp.sum(partials.astype(jnp.float32), axis=0)).astype(jnp.bfloat16)
    normed = rms_norm(attended, norm_gain)
    slot_total = N_EXPERT * CAP

    def per_expert(running, inputs):
        up_e, down_e, expert_index = inputs
        is_hit = expert_ids == expert_index
        chosen = jnp.any(is_hit, axis=1)
        gate_sum = lax.optimization_barrier(jnp.sum(jnp.where(is_hit, gate_values, 0.0), axis=1))
        picked = jnp.nonzero(chosen, size=slot_total, fill_value=0)[0].astype(jnp.int32)
        in_slot = jnp.arange(slot_total, dtype=jnp.int32) < jnp.sum(chosen.astype(jnp.int32))
        taken_rows = normed[picked]
        up_proj = jnp.dot(taken_rows, up_e, preferred_element_type=jnp.float32)
        hidden = jax.nn.silu(up_proj).astype(jnp.bfloat16)
        slice_parts = jnp.einsum('rtf,tfd->trd', hidden.reshape(slot_total, N_TENSOR, FF_DEV).astype(jnp.float32), down_e.reshape(N_TENSOR, FF_DEV, MODEL_WIDTH).astype(jnp.float32))
        slice_parts = slice_parts.astype(jnp.bfloat16)
        pair_out = lax.optimization_barrier(jnp.sum(slice_parts.astype(jnp.float32), axis=0)).astype(jnp.bfloat16)
        added = jnp.where(in_slot[:, None], gate_sum[picked][:, None] * pair_out.astype(jnp.float32), 0.0)
        return (running.at[picked].add(added), None)
    start = jnp.zeros((expert_ids.shape[0], MODEL_WIDTH), jnp.float32)
    indices = jnp.arange(N_EXPERT, dtype=jnp.int32)
    running, unused = lax.scan(per_expert, start, (up_weight, down_weight, indices))
    return running.astype(jnp.bfloat16)
```

```python
import functools

import jax
import jax.numpy as jnp
from jax import lax
from jax.experimental import pallas as pl
from jax.experimental.pallas import tpu as pltpu
from jax.sharding import PartitionSpec as P

CAP = 4
CUTS = 4
GRP = CAP * CUTS
MESH = pl.DeviceIdType.MESH
F32 = jnp.float32
BF16 = jnp.bfloat16


def iota(shape, dim):
    return lax.broadcasted_iota(jnp.int32, shape, dim)


def nt_dot(a, b):
    return lax.dot_general(a, b, (((1,), (1,)), ((), ())), preferred_element_type=F32)


def nn_dot(a, b):
    return jnp.dot(a, b, preferred_element_type=F32)


def kernel(
    dims,
    part_hbm,
    gain_hbm,
    ids_hbm,
    gate_hbm,
    up_hbm,
    down_hbm,
    out_ref,
    part_v,
    gain_v,
    ids_v,
    gate_v,
    up_v,
    down_v,
    gain_rows,
    spread,
    send1,
    recv1,
    send2,
    xbuf,
    send3,
    recv3,
    send4,
    recv4,
    recv5,
    load_sem,
    s1,
    r1,
    s2,
    r2,
    s2b,
    r2b,
    s3,
    r3,
    s4,
    r4,
    s5,
    r5,
):
    n_e, n_t, rows, width = dims
    ff = up_hbm.shape[2]
    chunk = width // CUTS
    lanes = send1.shape[2]
    picks = 2 * n_e
    crow = CUTS * picks
    own = rows // n_t
    srow = n_e * GRP
    me_e = lax.axis_index("expert")
    me_t = lax.axis_index("tensor")
    t_order = sorted(range(1, n_t), key=lambda j: -min(j, n_t - j))
    e_order = sorted(range(1, n_e), key=lambda j: -min(j, n_e - j))
    t_peers = [lax.rem(me_t + j, n_t) for j in t_order]
    e_peers = [lax.rem(me_e + j, n_e) for j in e_order]

    barrier = pltpu.get_barrier_semaphore()
    for peer in t_peers:
        pl.semaphore_signal(barrier, inc=1, device_id={"tensor": peer}, device_id_type=MESH)
    for peer in e_peers:
        pl.semaphore_signal(barrier, inc=1, device_id={"expert": peer}, device_id_type=MESH)

    small = [
        pltpu.make_async_copy(ids_hbm, ids_v, load_sem.at[0]),
        pltpu.make_async_copy(gate_hbm, gate_v, load_sem.at[1]),
    ]
    parts = [
        pltpu.make_async_copy(
            part_hbm.at[0, :, pl.ds(c * chunk, chunk)],
            part_v.at[pl.ds(c * rows, rows), :],
            load_sem.at[2 + c],
        )
        for c in range(CUTS)
    ]
    gain_copy = pltpu.make_async_copy(gain_hbm, gain_v, load_sem.at[2 + CUTS])
    ups = [
        pltpu.make_async_copy(
            up_hbm.at[0, pl.ds(c * chunk, chunk), :],
            up_v.at[:, pl.ds(c * ff, ff)],
            load_sem.at[3 + CUTS + c],
        )
        for c in range(CUTS)
    ]
    downs = [
        pltpu.make_async_copy(
            down_hbm.at[0, :, pl.ds(c * chunk, chunk)],
            down_v.at[pl.ds(c * ff, ff), :],
            load_sem.at[3 + 2 * CUTS + c],
        )
        for c in range(CUTS)
    ]
    for copy in small + parts + [gain_copy] + ups + downs:
        copy.start()
    for copy in small:
        copy.wait()

    slot_l = max(128, srow)
    pick_l = max(128, crow)
    lane = iota((rows, slot_l), 1)
    lane_e = lane // GRP
    lane_s = lane % CAP
    named = jnp.zeros((rows, slot_l), F32)
    gates = jnp.zeros((rows, slot_l), F32)
    for k in range(ids_v.shape[1]):
        hit = (ids_v[:, k : k + 1] == lane_e) & (lane < srow)
        named = named + jnp.where(hit, 1.0, 0.0)
        gates = gates + jnp.where(hit, gate_v[:, k : k + 1], 0.0)
    before = (iota((rows, rows), 0) > iota((rows, rows), 1)).astype(F32).astype(BF16)
    rank = nn_dot(before, named.astype(BF16)).astype(jnp.int32)
    in_slot = jnp.where(rank == lane_s, named, 0.0)
    slot_gate = in_slot * gates
    any_hit = jnp.broadcast_to(jnp.max(named, axis=1, keepdims=True), (rows, pick_l))
    place = nn_dot(before, any_hit.astype(BF16)).astype(jnp.int32)
    lane_p = iota((rows, pick_l), 1)
    picked = jnp.where((place == lane_p % picks) & (lane_p < crow), any_hit, 0.0).astype(BF16)
    spread[...] = picked.astype(F32)

    pick_row = (iota((crow, pick_l), 0) == iota((crow, pick_l), 1)).astype(F32).astype(BF16)
    pick_t = nt_dot(pick_row, picked)
    stacked = jnp.concatenate([picked] * CUTS, axis=0)
    wide = nt_dot(pick_row, stacked)
    chooser = jnp.where(
        iota((crow, CUTS * rows), 0) // picks == iota((crow, CUTS * rows), 1) // rows, wide, 0.0
    ).astype(BF16)

    for copy in parts:
        copy.wait()
    for t in range(n_t):
        lo, hi = min(t * lanes, chunk), min((t + 1) * lanes, chunk)
        if hi - lo < lanes:
            send1[t] = jnp.zeros((crow, lanes), BF16)
        if hi > lo:
            send1[t, :, : hi - lo] = nn_dot(chooser, part_v[:, lo:hi]).astype(BF16)

    pl.semaphore_wait(barrier, len(t_peers) + len(e_peers))

    def copy1(src_t, dst_t):
        return pltpu.make_async_remote_copy(
            src_ref=send1.at[dst_t],
            dst_ref=recv1.at[src_t],
            send_sem=s1.at[dst_t],
            recv_sem=r1.at[src_t],
            device_id={"tensor": dst_t},
            device_id_type=MESH,
        )

    for peer in t_peers:
        copy1(me_t, peer).start()

    slot_row = (iota((srow, slot_l), 0) == iota((srow, slot_l), 1)).astype(F32).astype(BF16)
    slot_t = nt_dot(slot_row, in_slot.astype(BF16)).astype(BF16)
    to_slots = nn_dot(slot_t, picked)
    to_slots = jnp.where(
        (iota((srow, pick_l), 0) % GRP) // CAP == iota((srow, pick_l), 1) // picks, to_slots, 0.0
    )[:, :crow].astype(BF16)
    mix = jnp.dot(pick_t, slot_gate, preferred_element_type=F32, precision=lax.Precision.HIGHEST)
    mix = jnp.where(
        iota((crow, slot_l), 0) // picks == (iota((crow, slot_l), 1) % GRP) // CAP, mix, 0.0
    )[:, :srow]
    mix_hi = mix.astype(BF16)
    mix_lo = (mix - mix_hi.astype(F32)).astype(BF16)
    gain_copy.wait()
    row_c = iota((GRP, chunk), 0) // CAP
    spread_gain = jnp.broadcast_to(gain_v[:, :chunk], (GRP, chunk))
    for c in range(1, CUTS):
        spread_gain = jnp.where(
            row_c == c,
            jnp.broadcast_to(gain_v[:, c * chunk : (c + 1) * chunk], (GRP, chunk)),
            spread_gain,
        )
    gain_rows[...] = spread_gain

    total = send1[me_t].astype(F32)
    for peer in t_peers:
        copy1(peer, me_t).wait_recv()
        total = total + recv1[peer].astype(F32)
    attended = total.astype(BF16)
    slots = nn_dot(to_slots, attended).astype(BF16)
    for e in range(n_e):
        send2[e] = slots[e * GRP : (e + 1) * GRP]

    def xpart(b, t):
        return xbuf.at[
            pl.ds(pl.multiple_of(b * GRP, GRP), GRP), pl.ds(pl.multiple_of(t * lanes, 128), lanes)
        ]

    def copy2(src_e, dst_e):
        return pltpu.make_async_remote_copy(
            src_ref=send2.at[dst_e],
            dst_ref=xpart(src_e, me_t),
            send_sem=s2.at[dst_e],
            recv_sem=r2.at[src_e],
            device_id={"expert": dst_e},
            device_id_type=MESH,
        )

    def copy2b(b, src_t, dst_t):
        return pltpu.make_async_remote_copy(
            src_ref=xpart(b, src_t),
            dst_ref=xpart(b, src_t),
            send_sem=s2b.at[b, dst_t],
            recv_sem=r2b.at[b, src_t],
            device_id={"tensor": dst_t},
            device_id_type=MESH,
        )

    for peer in e_peers:
        copy2(me_e, peer).start()
    xpart(me_e, me_t)[...] = send2[me_e]
    for peer in t_peers:
        copy2b(me_e, me_t, peer).start()
    for src in e_peers[::-1]:
        copy2(src, me_e).wait_recv()
        for peer in t_peers:
            copy2b(src, me_t, peer).start()
    for copy in ups:
        copy.wait()
    for src in t_peers[::-1]:
        for b in [me_e] + e_peers[::-1]:
            copy2b(b, src, me_t).wait_recv()

    rows_x = xbuf[:, :chunk].astype(F32)
    square = jnp.sum(rows_x * rows_x, axis=1, keepdims=True)
    scaled = (rows_x.reshape(n_e, GRP, chunk) * gain_rows[...][None]).reshape(srow, chunk)
    up_all = nn_dot(scaled.astype(BF16), up_v[...])
    own_c = (iota((srow, ff), 0) % GRP) // CAP
    up_own = up_all[:, :ff]
    for c in range(1, CUTS):
        up_own = jnp.where(own_c == c, up_all[:, c * ff : (c + 1) * ff], up_own)
    joined = jnp.concatenate([up_own, jnp.broadcast_to(square, (srow, ff))], axis=1)
    r_i, c_i = iota((srow, srow), 0), iota((srow, srow), 1)
    same = ((r_i // GRP == c_i // GRP) & (r_i % CAP == c_i % CAP)).astype(F32)
    summed = jnp.dot(same, joined, preferred_element_type=F32, precision=lax.Precision.HIGHEST)
    up_proj = summed[:, :ff] * lax.rsqrt(summed[:, ff:] * (1.0 / width) + 1e-06)
    hidden = up_proj / (1.0 + jnp.exp(-up_proj))
    spread_h = jnp.concatenate(
        [jnp.where(own_c == c, hidden, 0.0).astype(BF16) for c in range(CUTS)], axis=1
    )
    for copy in downs:
        copy.wait()

    def copy3(src_t, dst_t):
        return pltpu.make_async_remote_copy(
            src_ref=send3.at[dst_t],
            dst_ref=recv3.at[src_t],
            send_sem=s3.at[dst_t],
            recv_sem=r3.at[src_t],
            device_id={"tensor": dst_t},
            device_id_type=MESH,
        )

    for t in range(n_t):
        lo, hi = min(t * lanes, chunk), min((t + 1) * lanes, chunk)
        if hi - lo < lanes:
            send3[t] = jnp.zeros((srow, lanes), BF16)
        if hi > lo:
            send3[t, :, : hi - lo] = nn_dot(spread_h, down_v[:, lo:hi]).astype(BF16)
    for peer in t_peers:
        copy3(me_t, peer).start()

    total = send3[me_t].astype(F32)
    for peer in t_peers[::-1]:
        copy3(peer, me_t).wait_recv()
        total = total + recv3[peer].astype(F32)
    send4[...] = total.astype(BF16).reshape(n_e, GRP, lanes)

    def copy4(src_e, dst_e):
        return pltpu.make_async_remote_copy(
            src_ref=send4.at[dst_e],
            dst_ref=recv4.at[src_e],
            send_sem=s4.at[dst_e],
            recv_sem=r4.at[src_e],
            device_id={"expert": dst_e},
            device_id_type=MESH,
        )

    for peer in e_peers:
        copy4(me_e, peer).start()
    recv4[me_e] = send4[me_e]
    for peer in e_peers[::-1]:
        copy4(peer, me_e).wait_recv()
    pairs = recv4[...].reshape(srow, lanes)
    mixed = nn_dot(mix_hi, pairs) + nn_dot(mix_lo, pairs)
    recv5[me_t] = mixed.astype(BF16)

    def copy5(src_t, dst_t):
        return pltpu.make_async_remote_copy(
            src_ref=recv5.at[src_t],
            dst_ref=recv5.at[src_t],
            send_sem=s5.at[dst_t],
            recv_sem=r5.at[src_t],
            device_id={"tensor": dst_t},
            device_id_type=MESH,
        )

    for peer in t_peers:
        copy5(me_t, peer).start()

    mine = spread[pl.ds(pl.multiple_of(me_t * own, own), own), :]
    home = jnp.concatenate([mine] * CUTS, axis=0)
    home = jnp.where(
        iota((CUTS * own, pick_l), 0) // own == iota((CUTS * own, pick_l), 1) // picks, home, 0.0
    )[:, :crow].astype(BF16)
    for peer in t_peers[::-1]:
        copy5(peer, me_t).wait_recv()
    for t in range(n_t):
        lo, hi = min(t * lanes, chunk), min((t + 1) * lanes, chunk)
        if hi > lo:
            block = nn_dot(home, recv5[t]).astype(BF16)
            for c in range(CUTS):
                out_ref[:, c * chunk + lo : c * chunk + hi] = block[
                    c * own : (c + 1) * own, : hi - lo
                ]

    for peer in t_peers:
        copy1(me_t, peer).wait_send()
        copy3(me_t, peer).wait_send()
        copy5(me_t, peer).wait_send()
        for b in [me_e] + e_peers:
            copy2b(b, me_t, peer).wait_send()
    for peer in e_peers:
        copy2(me_e, peer).wait_send()
        copy4(me_e, peer).wait_send()


def on_device(partials, norm_gain, expert_ids, gate_values, up_weight, down_weight):
    n_e, n_t = lax.axis_size("expert"), lax.axis_size("tensor")
    rows, width = partials.shape[1:]
    ff = up_weight.shape[2]
    chunk = width // CUTS
    lanes = -(-(chunk // 128) // n_t) * 128
    crow = CUTS * 2 * n_e
    srow = n_e * GRP
    own = rows // n_t
    dma = pltpu.SemaphoreType.DMA
    return pl.pallas_call(
        functools.partial(kernel, (n_e, n_t, rows, width)),
        out_shape=jax.ShapeDtypeStruct((own, width), BF16),
        in_specs=[pl.BlockSpec(memory_space=pl.ANY)] * 6,
        out_specs=pl.BlockSpec(memory_space=pltpu.VMEM),
        scratch_shapes=[
            pltpu.VMEM((CUTS * rows, chunk), BF16),
            pltpu.VMEM((1, width), F32),
            pltpu.VMEM(expert_ids.shape, jnp.int32),
            pltpu.VMEM(gate_values.shape, F32),
            pltpu.VMEM((chunk, CUTS * ff), BF16),
            pltpu.VMEM((CUTS * ff, chunk), BF16),
            pltpu.VMEM((GRP, chunk), F32),
            pltpu.VMEM((rows, max(128, crow)), F32),
            pltpu.VMEM((n_t, crow, lanes), BF16),
            pltpu.VMEM((n_t, crow, lanes), BF16),
            pltpu.VMEM((n_e, GRP, lanes), BF16),
            pltpu.VMEM((srow, n_t * lanes), BF16),
            pltpu.VMEM((n_t, srow, lanes), BF16),
            pltpu.VMEM((n_t, srow, lanes), BF16),
            pltpu.VMEM((n_e, GRP, lanes), BF16),
            pltpu.VMEM((n_e, GRP, lanes), BF16),
            pltpu.VMEM((n_t, crow, lanes), BF16),
            dma((3 + 3 * CUTS,)),
            dma((n_t,)),
            dma((n_t,)),
            dma((n_e,)),
            dma((n_e,)),
            dma((n_e, n_t)),
            dma((n_e, n_t)),
            dma((n_t,)),
            dma((n_t,)),
            dma((n_e,)),
            dma((n_e,)),
            dma((n_t,)),
            dma((n_t,)),
        ],
        compiler_params=pltpu.CompilerParams(
            collective_id=0, has_side_effects=True, vmem_limit_bytes=48 * 1024 * 1024
        ),
    )(partials, norm_gain.reshape(1, width), expert_ids, gate_values, up_weight, down_weight)


def solution(mesh):
    in_specs = (
        P("tensor", ("groups", "expert"), None),
        P(),
        P(("groups", "expert"), None),
        P(("groups", "expert"), None),
        P("expert", None, "tensor"),
        P("expert", "tensor", None),
    )
    out_specs = P(("groups", "expert", "tensor"), None)
    return jax.shard_map(
        on_device, mesh=mesh, in_specs=in_specs, out_specs=out_specs, check_vma=False
    )
```

```python
import functools

import jax
import jax.numpy as jnp
from jax import lax
from jax.experimental import pallas as pl
from jax.experimental.pallas import tpu as pltpu
from jax.sharding import PartitionSpec as P

CAP = 4
CUTS = 4
GRP = CAP * CUTS
MESH = pl.DeviceIdType.MESH
F32 = jnp.float32
BF16 = jnp.bfloat16


def iota(shape, dim):
    return lax.broadcasted_iota(jnp.int32, shape, dim)


def div(x, n):
    return x >> (n.bit_length() - 1) if n & (n - 1) == 0 else x // n


def mod(x, n):
    return x & (n - 1) if n & (n - 1) == 0 else x % n


def nt_dot(a, b):
    return lax.dot_general(a, b, (((1,), (1,)), ((), ())), preferred_element_type=F32)


def nn_dot(a, b):
    return jnp.dot(a, b, preferred_element_type=F32)


def kernel(
    dims,
    part_hbm,
    gain_hbm,
    ids_hbm,
    gate_hbm,
    up_hbm,
    down_hbm,
    out_ref,
    part_v,
    gain_v,
    ids_v,
    gate_v,
    up_v,
    down_v,
    gain_rows,
    send1,
    recv1,
    send2,
    xbuf,
    send3,
    recv3,
    send4,
    recv4,
    recv5,
    load_sem,
    s1,
    r1,
    s2,
    r2,
    s2b,
    r2b,
    s3,
    r3,
    s4,
    r4,
    s5,
    r5,
):
    n_e, n_t, rows, width = dims
    ff = up_hbm.shape[2]
    chunk = width // CUTS
    lanes = send1.shape[2]
    picks = 2 * n_e
    crow = CUTS * picks
    own = rows // n_t
    srow = n_e * GRP
    me_e = lax.axis_index("expert")
    me_t = lax.axis_index("tensor")
    t_order = sorted(range(1, n_t), key=lambda j: -min(j, n_t - j))
    e_order = sorted(range(1, n_e), key=lambda j: -min(j, n_e - j))
    t_peers = [lax.rem(me_t + j, n_t) for j in t_order]
    e_peers = [lax.rem(me_e + j, n_e) for j in e_order]

    barrier = pltpu.get_barrier_semaphore()
    for peer in t_peers:
        pl.semaphore_signal(barrier, inc=1, device_id={"tensor": peer}, device_id_type=MESH)
    for peer in e_peers:
        pl.semaphore_signal(barrier, inc=1, device_id={"expert": peer}, device_id_type=MESH)

    small = [
        pltpu.make_async_copy(ids_hbm, ids_v, load_sem.at[0]),
        pltpu.make_async_copy(gate_hbm, gate_v, load_sem.at[1]),
    ]
    parts = [
        pltpu.make_async_copy(
            part_hbm.at[0, :, pl.ds(c * chunk, chunk)],
            part_v.at[pl.ds(c * rows, rows), :],
            load_sem.at[2 + c],
        )
        for c in range(CUTS)
    ]
    gain_copy = pltpu.make_async_copy(gain_hbm, gain_v, load_sem.at[2 + CUTS])
    ups = [
        pltpu.make_async_copy(
            up_hbm.at[0, pl.ds(c * chunk, chunk), :],
            up_v.at[:, pl.ds(c * ff, ff)],
            load_sem.at[3 + CUTS + c],
        )
        for c in range(CUTS)
    ]
    downs = [
        pltpu.make_async_copy(
            down_hbm.at[0, :, pl.ds(c * chunk, chunk)],
            down_v.at[pl.ds(c * ff, ff), :],
            load_sem.at[3 + 2 * CUTS + c],
        )
        for c in range(CUTS)
    ]
    for copy in small + parts + [gain_copy] + ups + downs:
        copy.start()
    for copy in small:
        copy.wait()

    slot_r = iota((srow, rows), 0)
    slot_e = div(slot_r, GRP)
    named = jnp.zeros((srow, rows), F32)
    gates = jnp.zeros((srow, rows), F32)
    for k in range(ids_v.shape[0]):
        hit = ids_v[k : k + 1, :] == slot_e
        named = jnp.where(hit, 1.0, named)
        gates = jnp.where(hit, gate_v[k : k + 1, :], gates)
    before = (iota((rows, rows), 0) < iota((rows, rows), 1)).astype(F32).astype(BF16)
    any_hit = jnp.broadcast_to(jnp.max(named, axis=0, keepdims=True), (crow, rows))
    counts = nn_dot(jnp.concatenate([any_hit, named], axis=0).astype(BF16), before)
    pick_r = mod(iota((crow, rows), 0), picks).astype(F32)
    picked = jnp.where(counts[:crow] == pick_r, any_hit, 0.0)
    pick_b = picked.astype(BF16)
    rank = counts[crow:]
    repeat = iota((rows, CUTS * rows), 0) == mod(iota((rows, CUTS * rows), 1), rows)
    wide = nn_dot(pick_b, repeat.astype(F32).astype(BF16))
    chooser = jnp.where(
        div(iota((crow, CUTS * rows), 0), picks) == div(iota((crow, CUTS * rows), 1), rows),
        wide,
        0.0,
    ).astype(BF16)

    for copy in parts:
        copy.wait()
    for t in range(n_t):
        lo, hi = min(t * lanes, chunk), min((t + 1) * lanes, chunk)
        if hi - lo < lanes:
            send1[t] = jnp.zeros((crow, lanes), BF16)
        if hi > lo:
            send1[t, :, : hi - lo] = nn_dot(chooser, part_v[:, lo:hi]).astype(BF16)

    pl.semaphore_wait(barrier, len(t_peers) + len(e_peers))

    def copy1(src_t, dst_t):
        return pltpu.make_async_remote_copy(
            src_ref=send1.at[dst_t],
            dst_ref=recv1.at[src_t],
            send_sem=s1.at[dst_t],
            recv_sem=r1.at[src_t],
            device_id={"tensor": dst_t},
            device_id_type=MESH,
        )

    for peer in t_peers:
        copy1(me_t, peer).start()

    in_slot = jnp.where(rank == mod(slot_r, CAP).astype(F32), named, 0.0)
    to_slots = jnp.where(
        div(mod(iota((srow, crow), 0), GRP), CAP) == div(iota((srow, crow), 1), picks),
        nt_dot(in_slot.astype(BF16), pick_b),
        0.0,
    ).astype(BF16)
    mix = lax.dot_general(
        picked,
        in_slot * gates,
        (((1,), (1,)), ((), ())),
        preferred_element_type=F32,
        precision=lax.Precision.HIGHEST,
    )
    mix = jnp.where(
        div(iota((crow, srow), 0), picks) == div(mod(iota((crow, srow), 1), GRP), CAP), mix, 0.0
    )
    mix_hi = mix.astype(BF16)
    mix_lo = (mix - mix_hi.astype(F32)).astype(BF16)
    home_r = iota((CUTS * own, rows), 0)
    mine = iota((CUTS * own, rows), 1) == mod(home_r, own) + me_t * own
    home = jnp.where(
        div(iota((CUTS * own, crow), 0), own) == div(iota((CUTS * own, crow), 1), picks),
        nt_dot(mine.astype(F32).astype(BF16), pick_b),
        0.0,
    ).astype(BF16)
    gain_copy.wait()
    row_c = div(iota((GRP, chunk), 0), CAP)
    spread_gain = jnp.broadcast_to(gain_v[:, :chunk], (GRP, chunk))
    for c in range(1, CUTS):
        spread_gain = jnp.where(
            row_c == c,
            jnp.broadcast_to(gain_v[:, c * chunk : (c + 1) * chunk], (GRP, chunk)),
            spread_gain,
        )
    gain_rows[...] = spread_gain

    total = send1[me_t].astype(F32)
    for peer in t_peers:
        copy1(peer, me_t).wait_recv()
        total = total + recv1[peer].astype(F32)
    attended = total.astype(BF16)
    slots = nn_dot(to_slots, attended).astype(BF16)
    for e in range(n_e):
        send2[e] = slots[e * GRP : (e + 1) * GRP]

    def xpart(b, t):
        return xbuf.at[
            pl.ds(pl.multiple_of(b * GRP, GRP), GRP), pl.ds(pl.multiple_of(t * lanes, 128), lanes)
        ]

    def copy2(src_e, dst_e):
        return pltpu.make_async_remote_copy(
            src_ref=send2.at[dst_e],
            dst_ref=xpart(src_e, me_t),
            send_sem=s2.at[dst_e],
            recv_sem=r2.at[src_e],
            device_id={"expert": dst_e},
            device_id_type=MESH,
        )

    def copy2b(b, src_t, dst_t):
        return pltpu.make_async_remote_copy(
            src_ref=xpart(b, src_t),
            dst_ref=xpart(b, src_t),
            send_sem=s2b.at[b, dst_t],
            recv_sem=r2b.at[b, src_t],
            device_id={"tensor": dst_t},
            device_id_type=MESH,
        )

    for peer in e_peers:
        copy2(me_e, peer).start()
    xpart(me_e, me_t)[...] = send2[me_e]
    for peer in t_peers:
        copy2b(me_e, me_t, peer).start()
    for src in e_peers[::-1]:
        copy2(src, me_e).wait_recv()
        for peer in t_peers:
            copy2b(src, me_t, peer).start()
    for copy in ups:
        copy.wait()
    for src in t_peers[::-1]:
        for b in [me_e] + e_peers[::-1]:
            copy2b(b, src, me_t).wait_recv()

    rows_x = xbuf[:, :chunk].astype(F32)
    square = jnp.sum(rows_x * rows_x, axis=1, keepdims=True)
    scaled = (rows_x.reshape(n_e, GRP, chunk) * gain_rows[...][None]).reshape(srow, chunk)
    up_all = nn_dot(scaled.astype(BF16), up_v[...])
    own_c = div(mod(iota((srow, ff), 0), GRP), CAP)
    up_own = up_all[:, :ff]
    for c in range(1, CUTS):
        up_own = jnp.where(own_c == c, up_all[:, c * ff : (c + 1) * ff], up_own)
    joined = jnp.concatenate([up_own, jnp.broadcast_to(square, (srow, ff))], axis=1)
    r_i, c_i = iota((srow, srow), 0), iota((srow, srow), 1)
    same = ((div(r_i, GRP) == div(c_i, GRP)) & (mod(r_i, CAP) == mod(c_i, CAP))).astype(F32)
    summed = jnp.dot(same, joined, preferred_element_type=F32, precision=lax.Precision.HIGHEST)
    up_proj = summed[:, :ff] * lax.rsqrt(summed[:, ff:] * (1.0 / width) + 1e-06)
    hidden = up_proj / (1.0 + jnp.exp(-up_proj))
    spread_h = jnp.concatenate(
        [jnp.where(own_c == c, hidden, 0.0).astype(BF16) for c in range(CUTS)], axis=1
    )
    for copy in downs:
        copy.wait()

    def copy3(src_t, dst_t):
        return pltpu.make_async_remote_copy(
            src_ref=send3.at[dst_t],
            dst_ref=recv3.at[src_t],
            send_sem=s3.at[dst_t],
            recv_sem=r3.at[src_t],
            device_id={"tensor": dst_t},
            device_id_type=MESH,
        )

    for t in range(n_t):
        lo, hi = min(t * lanes, chunk), min((t + 1) * lanes, chunk)
        if hi - lo < lanes:
            send3[t] = jnp.zeros((srow, lanes), BF16)
        if hi > lo:
            send3[t, :, : hi - lo] = nn_dot(spread_h, down_v[:, lo:hi]).astype(BF16)
    for peer in t_peers:
        copy3(me_t, peer).start()

    total = send3[me_t].astype(F32)
    for peer in t_peers[::-1]:
        copy3(peer, me_t).wait_recv()
        total = total + recv3[peer].astype(F32)
    send4[...] = total.astype(BF16).reshape(n_e, GRP, lanes)

    def copy4(src_e, dst_e):
        return pltpu.make_async_remote_copy(
            src_ref=send4.at[dst_e],
            dst_ref=recv4.at[src_e],
            send_sem=s4.at[dst_e],
            recv_sem=r4.at[src_e],
            device_id={"expert": dst_e},
            device_id_type=MESH,
        )

    for peer in e_peers:
        copy4(me_e, peer).start()
    recv4[me_e] = send4[me_e]
    for peer in e_peers[::-1]:
        copy4(peer, me_e).wait_recv()
    pairs = recv4[...].reshape(srow, lanes)
    mixed = nn_dot(mix_hi, pairs) + nn_dot(mix_lo, pairs)
    recv5[me_t] = mixed.astype(BF16)

    def copy5(src_t, dst_t):
        return pltpu.make_async_remote_copy(
            src_ref=recv5.at[src_t],
            dst_ref=recv5.at[src_t],
            send_sem=s5.at[dst_t],
            recv_sem=r5.at[src_t],
            device_id={"tensor": dst_t},
            device_id_type=MESH,
        )

    for peer in t_peers:
        copy5(me_t, peer).start()

    for peer in t_peers[::-1]:
        copy5(peer, me_t).wait_recv()
    for t in range(n_t):
        lo, hi = min(t * lanes, chunk), min((t + 1) * lanes, chunk)
        if hi > lo:
            block = nn_dot(home, recv5[t]).astype(BF16)
            for c in range(CUTS):
                out_ref[:, c * chunk + lo : c * chunk + hi] = block[
                    c * own : (c + 1) * own, : hi - lo
                ]

    for peer in t_peers:
        copy1(me_t, peer).wait_send()
        copy3(me_t, peer).wait_send()
        copy5(me_t, peer).wait_send()
        for b in [me_e] + e_peers:
            copy2b(b, me_t, peer).wait_send()
    for peer in e_peers:
        copy2(me_e, peer).wait_send()
        copy4(me_e, peer).wait_send()


def on_device(partials, norm_gain, expert_ids, gate_values, up_weight, down_weight):
    n_e, n_t = lax.axis_size("expert"), lax.axis_size("tensor")
    rows, width = partials.shape[1:]
    ff = up_weight.shape[2]
    chunk = width // CUTS
    lanes = -(-(chunk // 128) // n_t) * 128
    crow = CUTS * 2 * n_e
    srow = n_e * GRP
    own = rows // n_t
    dma = pltpu.SemaphoreType.DMA
    return pl.pallas_call(
        functools.partial(kernel, (n_e, n_t, rows, width)),
        out_shape=jax.ShapeDtypeStruct((own, width), BF16),
        in_specs=[pl.BlockSpec(memory_space=pl.ANY)] * 6,
        out_specs=pl.BlockSpec(memory_space=pltpu.VMEM),
        scratch_shapes=[
            pltpu.VMEM((CUTS * rows, chunk), BF16),
            pltpu.VMEM((1, width), F32),
            pltpu.VMEM(expert_ids.shape[::-1], jnp.int32),
            pltpu.VMEM(gate_values.shape[::-1], F32),
            pltpu.VMEM((chunk, CUTS * ff), BF16),
            pltpu.VMEM((CUTS * ff, chunk), BF16),
            pltpu.VMEM((GRP, chunk), F32),
            pltpu.VMEM((n_t, crow, lanes), BF16),
            pltpu.VMEM((n_t, crow, lanes), BF16),
            pltpu.VMEM((n_e, GRP, lanes), BF16),
            pltpu.VMEM((srow, n_t * lanes), BF16),
            pltpu.VMEM((n_t, srow, lanes), BF16),
            pltpu.VMEM((n_t, srow, lanes), BF16),
            pltpu.VMEM((n_e, GRP, lanes), BF16),
            pltpu.VMEM((n_e, GRP, lanes), BF16),
            pltpu.VMEM((n_t, crow, lanes), BF16),
            dma((3 + 3 * CUTS,)),
            dma((n_t,)),
            dma((n_t,)),
            dma((n_e,)),
            dma((n_e,)),
            dma((n_e, n_t)),
            dma((n_e, n_t)),
            dma((n_t,)),
            dma((n_t,)),
            dma((n_e,)),
            dma((n_e,)),
            dma((n_t,)),
            dma((n_t,)),
        ],
        compiler_params=pltpu.CompilerParams(
            collective_id=0, has_side_effects=True, vmem_limit_bytes=63 * 1024 * 1024
        ),
    )(partials, norm_gain.reshape(1, width), expert_ids.T, gate_values.T, up_weight, down_weight)


def solution(mesh):
    in_specs = (
        P("tensor", ("groups", "expert"), None),
        P(),
        P(("groups", "expert"), None),
        P(("groups", "expert"), None),
        P("expert", None, "tensor"),
        P("expert", "tensor", None),
    )
    out_specs = P(("groups", "expert", "tensor"), None)
    return jax.shard_map(
        on_device, mesh=mesh, in_specs=in_specs, out_specs=out_specs, check_vma=False
    )
```

```python
import functools

import jax
import jax.numpy as jnp
from jax import lax
from jax.experimental import pallas as pl
from jax.experimental.pallas import tpu as pltpu
from jax.sharding import PartitionSpec as P

CAP = 4
CUTS = 4
GRP = CAP * CUTS
MESH = pl.DeviceIdType.MESH
F32 = jnp.float32
BF16 = jnp.bfloat16


def iota(shape, dim):
    return lax.broadcasted_iota(jnp.int32, shape, dim)


def div(x, n):
    return x >> (n.bit_length() - 1) if n & (n - 1) == 0 else x // n


def mod(x, n):
    return x & (n - 1) if n & (n - 1) == 0 else x % n


def nt_dot(a, b):
    return lax.dot_general(a, b, (((1,), (1,)), ((), ())), preferred_element_type=F32)


def nn_dot(a, b):
    return jnp.dot(a, b, preferred_element_type=F32)


def kernel(
    dims,
    part_hbm,
    gain_hbm,
    ids_hbm,
    gate_hbm,
    up_hbm,
    down_hbm,
    out_ref,
    part_v,
    gain_v,
    ids_v,
    gate_v,
    up_v,
    down_v,
    gain_rows,
    send1,
    recv1,
    send2,
    xbuf,
    send3,
    recv3,
    send4,
    recv4,
    recv5,
    load_sem,
    s1,
    r1,
    s2,
    r2,
    s2b,
    r2b,
    s3,
    r3,
    s4,
    r4,
    s5,
    r5,
):
    n_e, n_t, rows, width = dims
    ff = up_hbm.shape[2]
    chunk = width // CUTS
    lanes = send1.shape[2]
    picks = 2 * n_e
    crow = CUTS * picks
    own = rows // n_t
    srow = n_e * GRP
    me_e = lax.axis_index("expert")
    me_t = lax.axis_index("tensor")
    n_x = n_t // 2
    core, me_x = lax.rem(me_t, 2), lax.div(me_t, 2)
    sibling = me_t + 1 - 2 * core
    t_order = sorted(range(1, n_t), key=lambda j: -min(j, n_t - j))
    e_order = sorted(range(1, n_e), key=lambda j: -min(j, n_e - j))
    t_peers = [lax.rem(me_t + j, n_t) for j in t_order]
    e_peers = [lax.rem(me_e + j, n_e) for j in e_order]
    x_peers = [lax.rem(me_x + j, n_x) for j in range(1, n_x)]
    far = [(e, x) for e in e_peers for x in x_peers + [me_x]] + [(me_e, x) for x in x_peers]

    barrier = pltpu.get_barrier_semaphore()
    for peer in t_peers:
        pl.semaphore_signal(barrier, inc=1, device_id={"tensor": peer}, device_id_type=MESH)
    for e in e_peers:
        for x in x_peers + [me_x]:
            pl.semaphore_signal(
                barrier,
                inc=1,
                device_id={"expert": e, "tensor": 2 * x + core},
                device_id_type=MESH,
            )

    small = [
        pltpu.make_async_copy(ids_hbm, ids_v, load_sem.at[0]),
        pltpu.make_async_copy(gate_hbm, gate_v, load_sem.at[1]),
    ]
    parts = [
        pltpu.make_async_copy(
            part_hbm.at[0, :, pl.ds(c * chunk, chunk)],
            part_v.at[pl.ds(c * rows, rows), pl.ds(0, chunk)],
            load_sem.at[2 + c],
        )
        for c in range(CUTS)
    ]
    gain_copy = pltpu.make_async_copy(gain_hbm, gain_v, load_sem.at[2 + CUTS])
    ups = [
        pltpu.make_async_copy(
            up_hbm.at[0, pl.ds(c * chunk, chunk), :],
            up_v.at[:, pl.ds(c * ff, ff)],
            load_sem.at[3 + CUTS + c],
        )
        for c in range(CUTS)
    ]
    downs = [
        pltpu.make_async_copy(
            down_hbm.at[0, :, pl.ds(c * chunk, chunk)],
            down_v.at[pl.ds(c * ff, ff), pl.ds(0, chunk)],
            load_sem.at[3 + 2 * CUTS + c],
        )
        for c in range(CUTS)
    ]
    for copy in small + parts:
        copy.start()
    pad = n_t * lanes - chunk
    part_v[:, chunk:] = jnp.zeros((CUTS * rows, pad), BF16)
    down_v[:, chunk:] = jnp.zeros((CUTS * ff, pad), BF16)
    for copy in small:
        copy.wait()

    slot_r = iota((srow, rows), 0)
    slot_e = div(slot_r, GRP)
    named = jnp.zeros((srow, rows), F32)
    gates = jnp.zeros((srow, rows), F32)
    for k in range(ids_v.shape[0]):
        hit = ids_v[k : k + 1, :] == slot_e
        named = jnp.where(hit, 1.0, named)
        gates = jnp.where(hit, gate_v[k : k + 1, :], gates)
    before = (iota((rows, rows), 0) < iota((rows, rows), 1)).astype(F32).astype(BF16)
    any_hit = jnp.broadcast_to(jnp.max(named, axis=0, keepdims=True), (crow, rows))
    counts = nn_dot(jnp.concatenate([any_hit, named], axis=0).astype(BF16), before)
    pick_r = mod(iota((crow, rows), 0), picks).astype(F32)
    picked = jnp.where(counts[:crow] == pick_r, any_hit, 0.0)
    pick_b = picked.astype(BF16)
    rank = counts[crow:]
    repeat = iota((rows, CUTS * rows), 0) == mod(iota((rows, CUTS * rows), 1), rows)
    wide = nn_dot(pick_b, repeat.astype(F32).astype(BF16))
    chooser = jnp.where(
        div(iota((crow, CUTS * rows), 0), picks) == div(iota((crow, CUTS * rows), 1), rows),
        wide,
        0.0,
    ).astype(BF16)

    for copy in parts:
        copy.wait()
    pl.semaphore_wait(barrier, len(t_peers) + len(e_peers) * n_x)

    def cols(t):
        return pl.ds(pl.multiple_of(t * lanes, 128), lanes)

    def copy1(src_t, dst_t):
        return pltpu.make_async_remote_copy(
            src_ref=send1.at[dst_t],
            dst_ref=recv1.at[src_t],
            send_sem=s1.at[dst_t],
            recv_sem=r1.at[src_t],
            device_id={"tensor": dst_t},
            device_id_type=MESH,
        )

    for peer in t_peers:
        send1[peer] = nn_dot(chooser, part_v[:, cols(peer)]).astype(BF16)
        copy1(me_t, peer).start()
    for copy in [gain_copy] + ups + downs:
        copy.start()
    total = nn_dot(chooser, part_v[:, cols(me_t)])

    in_slot = jnp.where(rank == mod(slot_r, CAP).astype(F32), named, 0.0)
    to_slots = jnp.where(
        div(mod(iota((srow, crow), 0), GRP), CAP) == div(iota((srow, crow), 1), picks),
        nt_dot(in_slot.astype(BF16), pick_b),
        0.0,
    ).astype(BF16)
    mix = lax.dot_general(
        picked,
        in_slot * gates,
        (((1,), (1,)), ((), ())),
        preferred_element_type=F32,
        precision=lax.Precision.HIGHEST,
    )
    mix = jnp.where(
        div(iota((crow, srow), 0), picks) == div(mod(iota((crow, srow), 1), GRP), CAP), mix, 0.0
    )
    mix_hi = mix.astype(BF16)
    mix_lo = (mix - mix_hi.astype(F32)).astype(BF16)
    home_r = iota((CUTS * own, rows), 0)
    mine = iota((CUTS * own, rows), 1) == mod(home_r, own) + me_t * own
    home = jnp.where(
        div(iota((CUTS * own, crow), 0), own) == div(iota((CUTS * own, crow), 1), picks),
        nt_dot(mine.astype(F32).astype(BF16), pick_b),
        0.0,
    ).astype(BF16)
    gain_copy.wait()
    row_c = div(iota((GRP, chunk), 0), CAP)
    spread_gain = jnp.broadcast_to(gain_v[:, :chunk], (GRP, chunk))
    for c in range(1, CUTS):
        spread_gain = jnp.where(
            row_c == c,
            jnp.broadcast_to(gain_v[:, c * chunk : (c + 1) * chunk], (GRP, chunk)),
            spread_gain,
        )
    gain_rows[...] = spread_gain

    for peer in t_peers:
        copy1(peer, me_t).wait_recv()
        total = total + recv1[peer].astype(F32)
    attended = total.astype(BF16)
    slots = nn_dot(to_slots, attended).astype(BF16)
    for e in range(n_e):
        send2[e] = slots[e * GRP : (e + 1) * GRP]

    def xpart(b, t):
        return xbuf.at[pl.ds(pl.multiple_of(b * GRP, GRP), GRP), cols(t)]

    def copy2(src_e, src_x, dst_e, dst_x):
        return pltpu.make_async_remote_copy(
            src_ref=send2.at[dst_e],
            dst_ref=xpart(src_e, 2 * src_x + core),
            send_sem=s2.at[dst_e, dst_x],
            recv_sem=r2.at[src_e, src_x],
            device_id={"expert": dst_e, "tensor": 2 * dst_x + core},
            device_id_type=MESH,
        )

    def copy2b(b, x, src_core):
        return pltpu.make_async_remote_copy(
            src_ref=xpart(b, 2 * x + src_core),
            dst_ref=xpart(b, 2 * x + src_core),
            send_sem=s2b.at[b, x],
            recv_sem=r2b.at[b, x],
            device_id={"tensor": sibling},
            device_id_type=MESH,
        )

    for e, x in far:
        copy2(me_e, me_x, e, x).start()
    xpart(me_e, me_t)[...] = send2[me_e]
    copy2b(me_e, me_x, core).start()
    for e, x in far[::-1]:
        copy2(e, x, me_e, me_x).wait_recv()
        copy2b(e, x, core).start()
    for copy in ups:
        copy.wait()
    for e, x in [(me_e, me_x)] + far[::-1]:
        copy2b(e, x, 1 - core).wait_recv()

    rows_x = xbuf[:, :chunk].astype(F32)
    square = jnp.sum(rows_x * rows_x, axis=1, keepdims=True)
    scaled = (rows_x.reshape(n_e, GRP, chunk) * gain_rows[...][None]).reshape(srow, chunk)
    up_all = nn_dot(scaled.astype(BF16), up_v[...])
    own_c = div(mod(iota((srow, ff), 0), GRP), CAP)
    up_own = up_all[:, :ff]
    for c in range(1, CUTS):
        up_own = jnp.where(own_c == c, up_all[:, c * ff : (c + 1) * ff], up_own)
    joined = jnp.concatenate([up_own, jnp.broadcast_to(square, (srow, ff))], axis=1)
    r_i, c_i = iota((srow, srow), 0), iota((srow, srow), 1)
    same = ((div(r_i, GRP) == div(c_i, GRP)) & (mod(r_i, CAP) == mod(c_i, CAP))).astype(F32)
    summed = jnp.dot(same, joined, preferred_element_type=F32, precision=lax.Precision.HIGHEST)
    up_proj = summed[:, :ff] * lax.rsqrt(summed[:, ff:] * (1.0 / width) + 1e-06)
    hidden = up_proj / (1.0 + jnp.exp(-up_proj))
    spread_h = jnp.concatenate(
        [jnp.where(own_c == c, hidden, 0.0).astype(BF16) for c in range(CUTS)], axis=1
    )
    for copy in downs:
        copy.wait()

    def copy3(x):
        return pltpu.make_async_remote_copy(
            src_ref=send3.at[x],
            dst_ref=recv3.at[x],
            send_sem=s3.at[x],
            recv_sem=r3.at[x],
            device_id={"tensor": sibling},
            device_id_type=MESH,
        )

    def copy4(src_e, src_x, dst_e, dst_x):
        return pltpu.make_async_remote_copy(
            src_ref=send4.at[dst_x, dst_e],
            dst_ref=recv4.at[src_x, src_e],
            send_sem=s4.at[dst_e, dst_x],
            recv_sem=r4.at[src_e, src_x],
            device_id={"expert": dst_e, "tensor": 2 * dst_x + core},
            device_id_type=MESH,
        )

    for x in x_peers + [me_x]:
        send3[x] = nn_dot(spread_h, down_v[:, cols(2 * x + 1 - core)]).astype(BF16)
        copy3(x).start()
    kept = [nn_dot(spread_h, down_v[:, cols(2 * x + core)]) for x in x_peers + [me_x]]
    for k, x in enumerate(x_peers + [me_x]):
        copy3(x).wait_recv()
        both = (kept[k] + recv3[x].astype(F32)).astype(BF16)
        send4[x] = both.reshape(n_e, GRP, lanes)
        for e in e_peers:
            copy4(me_e, me_x, e, x).start()
        if k < n_x - 1:
            copy4(me_e, me_x, me_e, x).start()
    recv4[me_x, me_e] = send4[me_x, me_e]
    for e, x in far[::-1]:
        copy4(e, x, me_e, me_x).wait_recv()
    pairs = jnp.sum(recv4[...].astype(F32), axis=0).astype(BF16).reshape(srow, lanes)
    mixed = nn_dot(mix_hi, pairs) + nn_dot(mix_lo, pairs)
    recv5[me_t] = mixed.astype(BF16)

    def copy5(src_t, dst_t):
        return pltpu.make_async_remote_copy(
            src_ref=recv5.at[src_t],
            dst_ref=recv5.at[src_t],
            send_sem=s5.at[dst_t],
            recv_sem=r5.at[src_t],
            device_id={"tensor": dst_t},
            device_id_type=MESH,
        )

    for peer in t_peers:
        copy5(me_t, peer).start()

    for peer in t_peers[::-1]:
        copy5(peer, me_t).wait_recv()
    for t in range(n_t):
        lo, hi = min(t * lanes, chunk), min((t + 1) * lanes, chunk)
        if hi > lo:
            block = nn_dot(home, recv5[t]).astype(BF16)
            for c in range(CUTS):
                out_ref[:, c * chunk + lo : c * chunk + hi] = block[
                    c * own : (c + 1) * own, : hi - lo
                ]

    for peer in t_peers:
        copy1(me_t, peer).wait_send()
        copy5(me_t, peer).wait_send()
    for x in x_peers + [me_x]:
        copy3(x).wait_send()
    copy2b(me_e, me_x, core).wait_send()
    for e, x in far:
        copy2(me_e, me_x, e, x).wait_send()
        copy2b(e, x, core).wait_send()
        copy4(me_e, me_x, e, x).wait_send()


def on_device(partials, norm_gain, expert_ids, gate_values, up_weight, down_weight):
    n_e, n_t = lax.axis_size("expert"), lax.axis_size("tensor")
    rows, width = partials.shape[1:]
    ff = up_weight.shape[2]
    chunk = width // CUTS
    lanes = -(-(chunk // 128) // n_t) * 128
    crow = CUTS * 2 * n_e
    srow = n_e * GRP
    own = rows // n_t
    n_x = n_t // 2
    dma = pltpu.SemaphoreType.DMA
    return pl.pallas_call(
        functools.partial(kernel, (n_e, n_t, rows, width)),
        out_shape=jax.ShapeDtypeStruct((own, width), BF16),
        in_specs=[pl.BlockSpec(memory_space=pl.ANY)] * 6,
        out_specs=pl.BlockSpec(memory_space=pltpu.VMEM),
        scratch_shapes=[
            pltpu.VMEM((CUTS * rows, n_t * lanes), BF16),
            pltpu.VMEM((1, width), F32),
            pltpu.VMEM(expert_ids.shape[::-1], jnp.int32),
            pltpu.VMEM(gate_values.shape[::-1], F32),
            pltpu.VMEM((chunk, CUTS * ff), BF16),
            pltpu.VMEM((CUTS * ff, n_t * lanes), BF16),
            pltpu.VMEM((GRP, chunk), F32),
            pltpu.VMEM((n_t, crow, lanes), BF16),
            pltpu.VMEM((n_t, crow, lanes), BF16),
            pltpu.VMEM((n_e, GRP, lanes), BF16),
            pltpu.VMEM((srow, n_t * lanes), BF16),
            pltpu.VMEM((n_x, srow, lanes), BF16),
            pltpu.VMEM((n_x, srow, lanes), BF16),
            pltpu.VMEM((n_x, n_e, GRP, lanes), BF16),
            pltpu.VMEM((n_x, n_e, GRP, lanes), BF16),
            pltpu.VMEM((n_t, crow, lanes), BF16),
            dma((3 + 3 * CUTS,)),
            dma((n_t,)),
            dma((n_t,)),
            dma((n_e, n_x)),
            dma((n_e, n_x)),
            dma((n_e, n_x)),
            dma((n_e, n_x)),
            dma((n_x,)),
            dma((n_x,)),
            dma((n_e, n_x)),
            dma((n_e, n_x)),
            dma((n_t,)),
            dma((n_t,)),
        ],
        compiler_params=pltpu.CompilerParams(
            collective_id=0, has_side_effects=True, vmem_limit_bytes=63 * 1024 * 1024
        ),
    )(partials, norm_gain.reshape(1, width), expert_ids.T, gate_values.T, up_weight, down_weight)


def solution(mesh):
    in_specs = (
        P("tensor", ("groups", "expert"), None),
        P(),
        P(("groups", "expert"), None),
        P(("groups", "expert"), None),
        P("expert", None, "tensor"),
        P("expert", "tensor", None),
    )
    out_specs = P(("groups", "expert", "tensor"), None)
    return jax.shard_map(
        on_device, mesh=mesh, in_specs=in_specs, out_specs=out_specs, check_vma=False
    )
```

```python
import functools

import jax
import jax.numpy as jnp
from jax import lax
from jax.experimental import pallas as pl
from jax.experimental.pallas import tpu as pltpu
from jax.sharding import PartitionSpec as P

CAP = 4
CUTS = 4
GRP = CAP * CUTS
MESH = pl.DeviceIdType.MESH
F32 = jnp.float32
BF16 = jnp.bfloat16


def iota(shape, dim):
    return lax.broadcasted_iota(jnp.int32, shape, dim)


def div(x, n):
    return x >> (n.bit_length() - 1) if n & (n - 1) == 0 else x // n


def mod(x, n):
    return x & (n - 1) if n & (n - 1) == 0 else x % n


def partners(me, n):
    if n & (n - 1):
        return [lax.rem(me + j, n) for j in range(n - 1, 0, -1)]
    flips = []
    for j in range(n - 1, 0, -1):
        other = me
        for b in range(n.bit_length() - 1):
            if j >> b & 1:
                other = other + (1 << b) * (1 - 2 * lax.rem(lax.div(me, 1 << b), 2))
        flips.append(other)
    return flips


def nt_dot(a, b):
    return lax.dot_general(a, b, (((1,), (1,)), ((), ())), preferred_element_type=F32)


def nn_dot(a, b):
    return jnp.dot(a, b, preferred_element_type=F32)


def kernel(
    dims,
    part_hbm,
    gain_hbm,
    ids_hbm,
    gate_hbm,
    up_hbm,
    down_hbm,
    out_ref,
    part_v,
    gain_v,
    ids_v,
    gate_v,
    up_v,
    down_v,
    gain_rows,
    send1,
    recv1,
    send2,
    xbuf,
    send3,
    recv3,
    send4,
    recv4,
    recv5,
    load_sem,
    s1,
    r1,
    s2,
    r2,
    s2b,
    r2b,
    s3,
    r3,
    s4,
    r4,
    s5,
    r5,
):
    n_e, n_t, rows, width = dims
    ff = up_hbm.shape[2]
    chunk = width // CUTS
    lanes = send1.shape[2]
    picks = 2 * n_e
    crow = CUTS * picks
    own = rows // n_t
    srow = n_e * GRP
    me_e = lax.axis_index("expert")
    me_t = lax.axis_index("tensor")
    n_x = n_t // 2
    core, me_x = lax.rem(me_t, 2), lax.div(me_t, 2)
    sibling = me_t + 1 - 2 * core
    t_peers = partners(me_t, n_t)
    e_peers = partners(me_e, n_e)
    x_peers = partners(me_x, n_x)
    far = [(e, x) for e in e_peers for x in x_peers + [me_x]] + [(me_e, x) for x in x_peers]

    barrier = pltpu.get_barrier_semaphore()
    for peer in t_peers:
        pl.semaphore_signal(barrier, inc=1, device_id={"tensor": peer}, device_id_type=MESH)
    for e in e_peers:
        for x in x_peers + [me_x]:
            pl.semaphore_signal(
                barrier,
                inc=1,
                device_id={"expert": e, "tensor": 2 * x + core},
                device_id_type=MESH,
            )

    small = [
        pltpu.make_async_copy(ids_hbm, ids_v, load_sem.at[0]),
        pltpu.make_async_copy(gate_hbm, gate_v, load_sem.at[1]),
    ]
    parts = [
        pltpu.make_async_copy(
            part_hbm.at[0, :, pl.ds(c * chunk, chunk)],
            part_v.at[pl.ds(c * rows, rows), pl.ds(0, chunk)],
            load_sem.at[2 + c],
        )
        for c in range(CUTS)
    ]
    gain_copy = pltpu.make_async_copy(gain_hbm, gain_v, load_sem.at[2 + CUTS])
    ups = [
        pltpu.make_async_copy(
            up_hbm.at[0, pl.ds(c * chunk, chunk), :],
            up_v.at[:, pl.ds(c * ff, ff)],
            load_sem.at[3 + CUTS + c],
        )
        for c in range(CUTS)
    ]
    downs = [
        pltpu.make_async_copy(
            down_hbm.at[0, :, pl.ds(c * chunk, chunk)],
            down_v.at[pl.ds(c * ff, ff), pl.ds(0, chunk)],
            load_sem.at[3 + 2 * CUTS + c],
        )
        for c in range(CUTS)
    ]
    for copy in small + parts:
        copy.start()
    pad = n_t * lanes - chunk
    part_v[:, chunk:] = jnp.zeros((CUTS * rows, pad), BF16)
    down_v[:, chunk:] = jnp.zeros((CUTS * ff, pad), BF16)
    for copy in small:
        copy.wait()

    slot_r = iota((srow, rows), 0)
    slot_e = div(slot_r, GRP)
    named = jnp.zeros((srow, rows), F32)
    gates = jnp.zeros((srow, rows), F32)
    for k in range(ids_v.shape[0]):
        hit = ids_v[k : k + 1, :] == slot_e
        named = jnp.where(hit, 1.0, named)
        gates = jnp.where(hit, gate_v[k : k + 1, :], gates)
    before = (iota((rows, rows), 0) < iota((rows, rows), 1)).astype(F32).astype(BF16)
    any_hit = jnp.broadcast_to(jnp.max(named, axis=0, keepdims=True), (crow, rows))
    counts = nn_dot(jnp.concatenate([any_hit, named], axis=0).astype(BF16), before)
    pick_r = mod(iota((crow, rows), 0), picks).astype(F32)
    picked = jnp.where(counts[:crow] == pick_r, any_hit, 0.0)
    pick_b = picked.astype(BF16)
    rank = counts[crow:]
    repeat = iota((rows, CUTS * rows), 0) == mod(iota((rows, CUTS * rows), 1), rows)
    wide = nn_dot(pick_b, repeat.astype(F32).astype(BF16))
    chooser = jnp.where(
        div(iota((crow, CUTS * rows), 0), picks) == div(iota((crow, CUTS * rows), 1), rows),
        wide,
        0.0,
    ).astype(BF16)

    for copy in parts:
        copy.wait()
    pl.semaphore_wait(barrier, len(t_peers) + len(e_peers) * n_x)

    def cols(t):
        place = lax.rem(t, 2) * n_x + lax.div(t, 2)
        return pl.ds(pl.multiple_of(place * lanes, 128), lanes)

    def copy1(src_t, dst_t):
        return pltpu.make_async_remote_copy(
            src_ref=send1.at[dst_t],
            dst_ref=recv1.at[src_t],
            send_sem=s1.at[dst_t],
            recv_sem=r1.at[src_t],
            device_id={"tensor": dst_t},
            device_id_type=MESH,
        )

    for peer in t_peers:
        send1[peer] = nn_dot(chooser, part_v[:, cols(peer)]).astype(BF16)
        copy1(me_t, peer).start()
    for copy in [gain_copy] + ups + downs:
        copy.start()
    total = nn_dot(chooser, part_v[:, cols(me_t)])

    in_slot = jnp.where(rank == mod(slot_r, CAP).astype(F32), named, 0.0)
    to_slots = jnp.where(
        div(mod(iota((srow, crow), 0), GRP), CAP) == div(iota((srow, crow), 1), picks),
        nt_dot(in_slot.astype(BF16), pick_b),
        0.0,
    ).astype(BF16)
    mix = lax.dot_general(
        picked,
        in_slot * gates,
        (((1,), (1,)), ((), ())),
        preferred_element_type=F32,
        precision=lax.Precision.HIGHEST,
    )
    mix = jnp.where(
        div(iota((crow, srow), 0), picks) == div(mod(iota((crow, srow), 1), GRP), CAP), mix, 0.0
    )
    mix_hi = mix.astype(BF16)
    mix_lo = (mix - mix_hi.astype(F32)).astype(BF16)
    home_r = iota((CUTS * own, rows), 0)
    mine = iota((CUTS * own, rows), 1) == mod(home_r, own) + me_t * own
    home = jnp.where(
        div(iota((CUTS * own, crow), 0), own) == div(iota((CUTS * own, crow), 1), picks),
        nt_dot(mine.astype(F32).astype(BF16), pick_b),
        0.0,
    ).astype(BF16)
    gain_copy.wait()
    row_c = div(iota((GRP, chunk), 0), CAP)
    spread_gain = jnp.broadcast_to(gain_v[:, :chunk], (GRP, chunk))
    for c in range(1, CUTS):
        spread_gain = jnp.where(
            row_c == c,
            jnp.broadcast_to(gain_v[:, c * chunk : (c + 1) * chunk], (GRP, chunk)),
            spread_gain,
        )
    gain_rows[...] = spread_gain

    for peer in t_peers:
        copy1(peer, me_t).wait_recv()
        total = total + recv1[peer].astype(F32)
    attended = total.astype(BF16)
    slots = nn_dot(to_slots, attended).astype(BF16)
    for e in range(n_e):
        send2[e] = slots[e * GRP : (e + 1) * GRP]

    def xpart(b, t):
        return xbuf.at[pl.ds(pl.multiple_of(b * GRP, GRP), GRP), cols(t)]

    def copy2(src_e, src_x, dst_e, dst_x):
        return pltpu.make_async_remote_copy(
            src_ref=send2.at[dst_e],
            dst_ref=xpart(src_e, 2 * src_x + core),
            send_sem=s2.at[dst_e, dst_x],
            recv_sem=r2.at[src_e, src_x],
            device_id={"expert": dst_e, "tensor": 2 * dst_x + core},
            device_id_type=MESH,
        )

    def copy2b(b, src_core):
        part = xbuf.at[
            pl.ds(pl.multiple_of(b * GRP, GRP), GRP),
            pl.ds(pl.multiple_of(src_core * n_x * lanes, 128), n_x * lanes),
        ]
        return pltpu.make_async_remote_copy(
            src_ref=part,
            dst_ref=part,
            send_sem=s2b.at[b],
            recv_sem=r2b.at[b],
            device_id={"tensor": sibling},
            device_id_type=MESH,
        )

    for e, x in far:
        copy2(me_e, me_x, e, x).start()
    xpart(me_e, me_t)[...] = send2[me_e]
    blocks = [me_e] + e_peers[::-1]
    for b in blocks:
        for x in x_peers[::-1] if b is me_e else [me_x] + x_peers[::-1]:
            copy2(b, x, me_e, me_x).wait_recv()
        copy2b(b, core).start()
    for copy in ups:
        copy.wait()
    for b in blocks:
        copy2b(b, 1 - core).wait_recv()

    rows_x = xbuf[:, :chunk].astype(F32)
    square = jnp.sum(rows_x * rows_x, axis=1, keepdims=True)
    scaled = (rows_x.reshape(n_e, GRP, chunk) * gain_rows[...][None]).reshape(srow, chunk)
    up_all = nn_dot(scaled.astype(BF16), up_v[...])
    own_c = div(mod(iota((srow, ff), 0), GRP), CAP)
    up_own = up_all[:, :ff]
    for c in range(1, CUTS):
        up_own = jnp.where(own_c == c, up_all[:, c * ff : (c + 1) * ff], up_own)
    joined = jnp.concatenate([up_own, jnp.broadcast_to(square, (srow, ff))], axis=1)
    r_i, c_i = iota((srow, srow), 0), iota((srow, srow), 1)
    same = ((div(r_i, GRP) == div(c_i, GRP)) & (mod(r_i, CAP) == mod(c_i, CAP))).astype(F32)
    summed = jnp.dot(same, joined, preferred_element_type=F32, precision=lax.Precision.HIGHEST)
    up_proj = summed[:, :ff] * lax.rsqrt(summed[:, ff:] * (1.0 / width) + 1e-06)
    hidden = up_proj / (1.0 + jnp.exp(-up_proj))
    spread_h = jnp.concatenate(
        [jnp.where(own_c == c, hidden, 0.0).astype(BF16) for c in range(CUTS)], axis=1
    )
    for copy in downs:
        copy.wait()

    def copy3(x):
        return pltpu.make_async_remote_copy(
            src_ref=send3.at[x],
            dst_ref=recv3.at[x],
            send_sem=s3.at[x],
            recv_sem=r3.at[x],
            device_id={"tensor": sibling},
            device_id_type=MESH,
        )

    def copy4(src_e, src_x, dst_e, dst_x):
        return pltpu.make_async_remote_copy(
            src_ref=send4.at[dst_x, dst_e],
            dst_ref=recv4.at[src_x, src_e],
            send_sem=s4.at[dst_e, dst_x],
            recv_sem=r4.at[src_e, src_x],
            device_id={"expert": dst_e, "tensor": 2 * dst_x + core},
            device_id_type=MESH,
        )

    for x in x_peers + [me_x]:
        send3[x] = nn_dot(spread_h, down_v[:, cols(2 * x + 1 - core)]).astype(BF16)
        copy3(x).start()
    kept = [nn_dot(spread_h, down_v[:, cols(2 * x + core)]) for x in x_peers + [me_x]]
    for k, x in enumerate(x_peers + [me_x]):
        copy3(x).wait_recv()
        both = (kept[k] + recv3[x].astype(F32)).astype(BF16)
        send4[x] = both.reshape(n_e, GRP, lanes)
        for e in e_peers:
            copy4(me_e, me_x, e, x).start()
        if k < n_x - 1:
            copy4(me_e, me_x, me_e, x).start()
    recv4[me_x, me_e] = send4[me_x, me_e]
    for e, x in far[::-1]:
        copy4(e, x, me_e, me_x).wait_recv()
    pairs = jnp.sum(recv4[...].astype(F32), axis=0).astype(BF16).reshape(srow, lanes)
    mixed = nn_dot(mix_hi, pairs) + nn_dot(mix_lo, pairs)
    recv5[me_t] = mixed.astype(BF16)

    def copy5(src_t, dst_t):
        return pltpu.make_async_remote_copy(
            src_ref=recv5.at[src_t],
            dst_ref=recv5.at[src_t],
            send_sem=s5.at[dst_t],
            recv_sem=r5.at[src_t],
            device_id={"tensor": dst_t},
            device_id_type=MESH,
        )

    for peer in t_peers:
        copy5(me_t, peer).start()

    for peer in t_peers[::-1]:
        copy5(peer, me_t).wait_recv()
    for t in range(n_t):
        place = t % 2 * n_x + t // 2
        lo, hi = min(place * lanes, chunk), min((place + 1) * lanes, chunk)
        if hi > lo:
            block = nn_dot(home, recv5[t]).astype(BF16)
            for c in range(CUTS):
                out_ref[:, c * chunk + lo : c * chunk + hi] = block[
                    c * own : (c + 1) * own, : hi - lo
                ]

    for peer in t_peers:
        copy1(me_t, peer).wait_send()
        copy5(me_t, peer).wait_send()
    for x in x_peers + [me_x]:
        copy3(x).wait_send()
    for b in blocks:
        copy2b(b, core).wait_send()
    for e, x in far:
        copy2(me_e, me_x, e, x).wait_send()
        copy4(me_e, me_x, e, x).wait_send()


def on_device(partials, norm_gain, expert_ids, gate_values, up_weight, down_weight):
    n_e, n_t = lax.axis_size("expert"), lax.axis_size("tensor")
    rows, width = partials.shape[1:]
    ff = up_weight.shape[2]
    chunk = width // CUTS
    lanes = -(-(chunk // 128) // n_t) * 128
    crow = CUTS * 2 * n_e
    srow = n_e * GRP
    own = rows // n_t
    n_x = n_t // 2
    dma = pltpu.SemaphoreType.DMA
    return pl.pallas_call(
        functools.partial(kernel, (n_e, n_t, rows, width)),
        out_shape=jax.ShapeDtypeStruct((own, width), BF16),
        in_specs=[pl.BlockSpec(memory_space=pl.ANY)] * 6,
        out_specs=pl.BlockSpec(memory_space=pltpu.VMEM),
        scratch_shapes=[
            pltpu.VMEM((CUTS * rows, n_t * lanes), BF16),
            pltpu.VMEM((1, width), F32),
            pltpu.VMEM(expert_ids.shape[::-1], jnp.int32),
            pltpu.VMEM(gate_values.shape[::-1], F32),
            pltpu.VMEM((chunk, CUTS * ff), BF16),
            pltpu.VMEM((CUTS * ff, n_t * lanes), BF16),
            pltpu.VMEM((GRP, chunk), F32),
            pltpu.VMEM((n_t, crow, lanes), BF16),
            pltpu.VMEM((n_t, crow, lanes), BF16),
            pltpu.VMEM((n_e, GRP, lanes), BF16),
            pltpu.VMEM((srow, n_t * lanes), BF16),
            pltpu.VMEM((n_x, srow, lanes), BF16),
            pltpu.VMEM((n_x, srow, lanes), BF16),
            pltpu.VMEM((n_x, n_e, GRP, lanes), BF16),
            pltpu.VMEM((n_x, n_e, GRP, lanes), BF16),
            pltpu.VMEM((n_t, crow, lanes), BF16),
            dma((3 + 3 * CUTS,)),
            dma((n_t,)),
            dma((n_t,)),
            dma((n_e, n_x)),
            dma((n_e, n_x)),
            dma((n_e,)),
            dma((n_e,)),
            dma((n_x,)),
            dma((n_x,)),
            dma((n_e, n_x)),
            dma((n_e, n_x)),
            dma((n_t,)),
            dma((n_t,)),
        ],
        compiler_params=pltpu.CompilerParams(
            collective_id=0, has_side_effects=True, vmem_limit_bytes=63 * 1024 * 1024
        ),
    )(partials, norm_gain.reshape(1, width), expert_ids.T, gate_values.T, up_weight, down_weight)


def solution(mesh):
    in_specs = (
        P("tensor", ("groups", "expert"), None),
        P(),
        P(("groups", "expert"), None),
        P(("groups", "expert"), None),
        P("expert", None, "tensor"),
        P("expert", "tensor", None),
    )
    out_specs = P(("groups", "expert", "tensor"), None)
    return jax.shard_map(
        on_device, mesh=mesh, in_specs=in_specs, out_specs=out_specs, check_vma=False
    )
```

```python
import functools

import jax
import jax.numpy as jnp
from jax import lax
from jax.experimental import pallas as pl
from jax.experimental.pallas import tpu as pltpu
from jax.sharding import PartitionSpec as P

CAP = 4
CUTS = 4
GRP = CAP * CUTS
MESH = pl.DeviceIdType.MESH
F32 = jnp.float32
BF16 = jnp.bfloat16


def iota(shape, dim):
    return lax.broadcasted_iota(jnp.int32, shape, dim)


def div(x, n):
    return x >> (n.bit_length() - 1) if n & (n - 1) == 0 else x // n


def mod(x, n):
    return x & (n - 1) if n & (n - 1) == 0 else x % n


def partners(me, n):
    if n & (n - 1):
        return [lax.rem(me + j, n) for j in range(n - 1, 0, -1)]
    flips = []
    for j in range(n - 1, 0, -1):
        other = me
        for b in range(n.bit_length() - 1):
            if j >> b & 1:
                other = other + (1 << b) * (1 - 2 * lax.rem(lax.div(me, 1 << b), 2))
        flips.append(other)
    return flips


def nt_dot(a, b):
    return lax.dot_general(a, b, (((1,), (1,)), ((), ())), preferred_element_type=F32)


def nn_dot(a, b):
    return jnp.dot(a, b, preferred_element_type=F32)


def kernel(
    dims,
    part_hbm,
    gain_hbm,
    ids_hbm,
    gate_hbm,
    up_hbm,
    down_hbm,
    out_ref,
    part_v,
    gain_v,
    ids_v,
    gate_v,
    up_v,
    down_v,
    gain_rows,
    send1,
    recv1,
    send2,
    xbuf,
    send3,
    recv3,
    send4,
    recv4,
    recv5,
    load_sem,
    s1,
    r1,
    s2,
    r2,
    s2b,
    r2b,
    s3,
    r3,
    s4,
    r4,
    s5,
    r5,
):
    n_e, n_t, rows, width = dims
    ff = up_hbm.shape[2]
    chunk = width // CUTS
    lanes = send1.shape[2]
    picks = 2 * n_e
    crow = CUTS * picks
    own = rows // n_t
    srow = n_e * GRP
    me_e = lax.axis_index("expert")
    me_t = lax.axis_index("tensor")
    n_x = n_t // 2
    core, me_x = lax.rem(me_t, 2), lax.div(me_t, 2)
    sibling = me_t + 1 - 2 * core
    t_peers = partners(me_t, n_t)
    e_peers = partners(me_e, n_e)
    x_peers = partners(me_x, n_x)
    far = [(e, x) for e in e_peers for x in x_peers + [me_x]] + [(me_e, x) for x in x_peers]

    small = [
        pltpu.make_async_copy(ids_hbm, ids_v, load_sem.at[0]),
        pltpu.make_async_copy(gate_hbm, gate_v, load_sem.at[1]),
    ]
    parts = [
        pltpu.make_async_copy(
            part_hbm.at[0, :, pl.ds(c * chunk, chunk)],
            part_v.at[pl.ds(c * rows, rows), pl.ds(0, chunk)],
            load_sem.at[2 + c],
        )
        for c in range(CUTS)
    ]
    gain_copy = pltpu.make_async_copy(gain_hbm, gain_v, load_sem.at[2 + CUTS])
    ups = [
        pltpu.make_async_copy(
            up_hbm.at[0, pl.ds(c * chunk, chunk), :],
            up_v.at[:, pl.ds(c * ff, ff)],
            load_sem.at[3 + CUTS + c],
        )
        for c in range(CUTS)
    ]
    downs = [
        pltpu.make_async_copy(
            down_hbm.at[0, :, pl.ds(c * chunk, chunk)],
            down_v.at[pl.ds(c * ff, ff), pl.ds(0, chunk)],
            load_sem.at[3 + 2 * CUTS + c],
        )
        for c in range(CUTS)
    ]
    for copy in small + parts:
        copy.start()

    barrier = pltpu.get_barrier_semaphore()
    for peer in t_peers:
        pl.semaphore_signal(barrier, inc=1, device_id={"tensor": peer}, device_id_type=MESH)
    for e in e_peers:
        for x in x_peers + [me_x]:
            pl.semaphore_signal(
                barrier,
                inc=1,
                device_id={"expert": e, "tensor": 2 * x + core},
                device_id_type=MESH,
            )

    pad = n_t * lanes - chunk
    part_v[:, chunk:] = jnp.zeros((CUTS * rows, pad), BF16)
    down_v[:, chunk:] = jnp.zeros((CUTS * ff, pad), BF16)
    for copy in small:
        copy.wait()

    slot_r = iota((srow, rows), 0)
    slot_e = div(slot_r, GRP)
    named = jnp.zeros((srow, rows), F32)
    gates = jnp.zeros((srow, rows), F32)
    for k in range(ids_v.shape[0]):
        hit = ids_v[k : k + 1, :] == slot_e
        named = jnp.where(hit, 1.0, named)
        gates = jnp.where(hit, gate_v[k : k + 1, :], gates)
    before = (iota((rows, rows), 0) < iota((rows, rows), 1)).astype(F32).astype(BF16)
    any_hit = jnp.broadcast_to(jnp.max(named, axis=0, keepdims=True), (crow, rows))
    counts = nn_dot(jnp.concatenate([any_hit, named], axis=0).astype(BF16), before)
    pick_r = mod(iota((crow, rows), 0), picks).astype(F32)
    picked = jnp.where(counts[:crow] == pick_r, any_hit, 0.0)
    pick_b = picked.astype(BF16)
    rank = counts[crow:]
    wide = jnp.concatenate([picked] * CUTS, axis=1)
    chooser = jnp.where(
        div(iota((crow, CUTS * rows), 0), picks) == div(iota((crow, CUTS * rows), 1), rows),
        wide,
        0.0,
    ).astype(BF16)

    for copy in parts:
        copy.wait()
    pl.semaphore_wait(barrier, len(t_peers) + len(e_peers) * n_x)

    def cols(t):
        place = lax.rem(t, 2) * n_x + lax.div(t, 2)
        return pl.ds(pl.multiple_of(place * lanes, 128), lanes)

    def copy1(src_t, dst_t):
        return pltpu.make_async_remote_copy(
            src_ref=send1.at[dst_t],
            dst_ref=recv1.at[src_t],
            send_sem=s1.at[dst_t],
            recv_sem=r1.at[src_t],
            device_id={"tensor": dst_t},
            device_id_type=MESH,
        )

    for peer in t_peers:
        send1[peer] = nn_dot(chooser, part_v[:, cols(peer)]).astype(BF16)
        copy1(me_t, peer).start()
    for copy in [gain_copy] + ups + downs:
        copy.start()
    total = nn_dot(chooser, part_v[:, cols(me_t)])

    in_slot = jnp.where(rank == mod(slot_r, CAP).astype(F32), named, 0.0)
    to_slots = jnp.where(
        div(mod(iota((srow, crow), 0), GRP), CAP) == div(iota((srow, crow), 1), picks),
        nt_dot(in_slot.astype(BF16), pick_b),
        0.0,
    ).astype(BF16)
    mix = lax.dot_general(
        picked,
        in_slot * gates,
        (((1,), (1,)), ((), ())),
        preferred_element_type=F32,
        precision=lax.Precision.HIGHEST,
    )
    mix = jnp.where(
        div(iota((crow, srow), 0), picks) == div(mod(iota((crow, srow), 1), GRP), CAP), mix, 0.0
    )
    mix_hi = mix.astype(BF16)
    mix_lo = mix - mix_hi.astype(F32)
    mix_two = jnp.concatenate([mix_hi.astype(F32), mix_lo], axis=1).astype(BF16)
    home_r = iota((CUTS * own, rows), 0)
    mine = iota((CUTS * own, rows), 1) == mod(home_r, own) + me_t * own
    home = jnp.where(
        div(iota((CUTS * own, crow), 0), own) == div(iota((CUTS * own, crow), 1), picks),
        nt_dot(mine.astype(F32).astype(BF16), pick_b),
        0.0,
    ).astype(BF16)
    gain_copy.wait()
    row_c = div(iota((GRP, chunk), 0), CAP)
    spread_gain = jnp.broadcast_to(gain_v[:, :chunk], (GRP, chunk))
    for c in range(1, CUTS):
        spread_gain = jnp.where(
            row_c == c,
            jnp.broadcast_to(gain_v[:, c * chunk : (c + 1) * chunk], (GRP, chunk)),
            spread_gain,
        )
    gain_rows[...] = spread_gain

    for peer in t_peers:
        copy1(peer, me_t).wait_recv()
        total = total + recv1[peer].astype(F32)
    attended = total.astype(BF16)
    slots = nn_dot(to_slots, attended).astype(BF16)
    for e in range(n_e):
        send2[e] = slots[e * GRP : (e + 1) * GRP]

    def xpart(b, t):
        return xbuf.at[pl.ds(pl.multiple_of(b * GRP, GRP), GRP), cols(t)]

    def copy2(src_e, src_x, dst_e, dst_x):
        return pltpu.make_async_remote_copy(
            src_ref=send2.at[dst_e],
            dst_ref=xpart(src_e, 2 * src_x + core),
            send_sem=s2.at[dst_e, dst_x],
            recv_sem=r2.at[src_e, src_x],
            device_id={"expert": dst_e, "tensor": 2 * dst_x + core},
            device_id_type=MESH,
        )

    def copy2b(b, src_core):
        part = xbuf.at[
            pl.ds(pl.multiple_of(b * GRP, GRP), GRP),
            pl.ds(pl.multiple_of(src_core * n_x * lanes, 128), n_x * lanes),
        ]
        return pltpu.make_async_remote_copy(
            src_ref=part,
            dst_ref=part,
            send_sem=s2b.at[b],
            recv_sem=r2b.at[b],
            device_id={"tensor": sibling},
            device_id_type=MESH,
        )

    for e, x in far:
        copy2(me_e, me_x, e, x).start()
    xpart(me_e, me_t)[...] = send2[me_e]
    blocks = [me_e] + e_peers[::-1]
    for b in blocks:
        for x in x_peers[::-1] if b is me_e else [me_x] + x_peers[::-1]:
            copy2(b, x, me_e, me_x).wait_recv()
        copy2b(b, core).start()
    for copy in ups:
        copy.wait()
    for b in blocks:
        copy2b(b, 1 - core).wait_recv()

    rows_x = xbuf[:, :chunk].astype(F32)
    square = jnp.sum(rows_x * rows_x, axis=1, keepdims=True)
    scaled = (rows_x.reshape(n_e, GRP, chunk) * gain_rows[...][None]).reshape(srow, chunk)
    up_all = nn_dot(scaled.astype(BF16), up_v[...])
    own_c = div(mod(iota((srow, ff), 0), GRP), CAP)
    up_own = up_all[:, :ff]
    for c in range(1, CUTS):
        up_own = jnp.where(own_c == c, up_all[:, c * ff : (c + 1) * ff], up_own)
    joined = jnp.concatenate([up_own, jnp.broadcast_to(square, (srow, ff))], axis=1)
    r_i, c_i = iota((srow, srow), 0), iota((srow, srow), 1)
    same = ((div(r_i, GRP) == div(c_i, GRP)) & (mod(r_i, CAP) == mod(c_i, CAP))).astype(F32)
    summed = jnp.dot(same, joined, preferred_element_type=F32, precision=lax.Precision.HIGHEST)
    up_proj = summed[:, :ff] * lax.rsqrt(summed[:, ff:] * (1.0 / width) + 1e-06)
    hidden = up_proj / (1.0 + jnp.exp(-up_proj))
    spread_h = jnp.concatenate(
        [jnp.where(own_c == c, hidden, 0.0).astype(BF16) for c in range(CUTS)], axis=1
    )
    for copy in downs:
        copy.wait()

    def copy3(x):
        return pltpu.make_async_remote_copy(
            src_ref=send3.at[x],
            dst_ref=recv3.at[x],
            send_sem=s3.at[x],
            recv_sem=r3.at[x],
            device_id={"tensor": sibling},
            device_id_type=MESH,
        )

    def copy4(src_e, src_x, dst_e, dst_x):
        return pltpu.make_async_remote_copy(
            src_ref=send4.at[dst_x, dst_e],
            dst_ref=recv4.at[src_x, src_e],
            send_sem=s4.at[dst_e, dst_x],
            recv_sem=r4.at[src_e, src_x],
            device_id={"expert": dst_e, "tensor": 2 * dst_x + core},
            device_id_type=MESH,
        )

    for x in x_peers + [me_x]:
        send3[x] = nn_dot(spread_h, down_v[:, cols(2 * x + 1 - core)]).astype(BF16)
        copy3(x).start()
    kept = [nn_dot(spread_h, down_v[:, cols(2 * x + core)]) for x in x_peers + [me_x]]
    for k, x in enumerate(x_peers + [me_x]):
        copy3(x).wait_recv()
        both = (kept[k] + recv3[x].astype(F32)).astype(BF16)
        send4[x] = both.reshape(n_e, GRP, lanes)
        for e in e_peers:
            copy4(me_e, me_x, e, x).start()
        if k < n_x - 1:
            copy4(me_e, me_x, me_e, x).start()
    recv4[me_x, me_e] = send4[me_x, me_e]
    for e, x in far[::-1]:
        copy4(e, x, me_e, me_x).wait_recv()
    pairs = jnp.sum(recv4[...].astype(F32), axis=0).astype(BF16).reshape(srow, lanes)
    mixed = nn_dot(mix_two, jnp.concatenate([pairs, pairs], axis=0))
    recv5[me_t] = mixed.astype(BF16)

    def copy5(src_t, dst_t):
        return pltpu.make_async_remote_copy(
            src_ref=recv5.at[src_t],
            dst_ref=recv5.at[src_t],
            send_sem=s5.at[dst_t],
            recv_sem=r5.at[src_t],
            device_id={"tensor": dst_t},
            device_id_type=MESH,
        )

    for peer in t_peers:
        copy5(me_t, peer).start()

    for peer in t_peers[::-1]:
        copy5(peer, me_t).wait_recv()
    for t in range(n_t):
        place = t % 2 * n_x + t // 2
        lo, hi = min(place * lanes, chunk), min((place + 1) * lanes, chunk)
        if hi > lo:
            block = nn_dot(home, recv5[t]).astype(BF16)
            for c in range(CUTS):
                out_ref[:, c * chunk + lo : c * chunk + hi] = block[
                    c * own : (c + 1) * own, : hi - lo
                ]

    for peer in t_peers:
        copy1(me_t, peer).wait_send()
        copy5(me_t, peer).wait_send()
    for x in x_peers + [me_x]:
        copy3(x).wait_send()
    for b in blocks:
        copy2b(b, core).wait_send()
    for e, x in far:
        copy2(me_e, me_x, e, x).wait_send()
        copy4(me_e, me_x, e, x).wait_send()


def on_device(partials, norm_gain, expert_ids, gate_values, up_weight, down_weight):
    n_e, n_t = lax.axis_size("expert"), lax.axis_size("tensor")
    rows, width = partials.shape[1:]
    ff = up_weight.shape[2]
    chunk = width // CUTS
    lanes = -(-(chunk // 128) // n_t) * 128
    crow = CUTS * 2 * n_e
    srow = n_e * GRP
    own = rows // n_t
    n_x = n_t // 2
    dma = pltpu.SemaphoreType.DMA
    return pl.pallas_call(
        functools.partial(kernel, (n_e, n_t, rows, width)),
        out_shape=jax.ShapeDtypeStruct((own, width), BF16),
        in_specs=[pl.BlockSpec(memory_space=pl.ANY)] * 6,
        out_specs=pl.BlockSpec(memory_space=pltpu.VMEM),
        scratch_shapes=[
            pltpu.VMEM((CUTS * rows, n_t * lanes), BF16),
            pltpu.VMEM((1, width), F32),
            pltpu.VMEM(expert_ids.shape[::-1], jnp.int32),
            pltpu.VMEM(gate_values.shape[::-1], F32),
            pltpu.VMEM((chunk, CUTS * ff), BF16),
            pltpu.VMEM((CUTS * ff, n_t * lanes), BF16),
            pltpu.VMEM((GRP, chunk), F32),
            pltpu.VMEM((n_t, crow, lanes), BF16),
            pltpu.VMEM((n_t, crow, lanes), BF16),
            pltpu.VMEM((n_e, GRP, lanes), BF16),
            pltpu.VMEM((srow, n_t * lanes), BF16),
            pltpu.VMEM((n_x, srow, lanes), BF16),
            pltpu.VMEM((n_x, srow, lanes), BF16),
            pltpu.VMEM((n_x, n_e, GRP, lanes), BF16),
            pltpu.VMEM((n_x, n_e, GRP, lanes), BF16),
            pltpu.VMEM((n_t, crow, lanes), BF16),
            dma((3 + 3 * CUTS,)),
            dma((n_t,)),
            dma((n_t,)),
            dma((n_e, n_x)),
            dma((n_e, n_x)),
            dma((n_e,)),
            dma((n_e,)),
            dma((n_x,)),
            dma((n_x,)),
            dma((n_e, n_x)),
            dma((n_e, n_x)),
            dma((n_t,)),
            dma((n_t,)),
        ],
        compiler_params=pltpu.CompilerParams(
            collective_id=0, has_side_effects=True, vmem_limit_bytes=63 * 1024 * 1024
        ),
    )(partials, norm_gain.reshape(1, width), expert_ids.T, gate_values.T, up_weight, down_weight)


def solution(mesh):
    in_specs = (
        P("tensor", ("groups", "expert"), None),
        P(),
        P(("groups", "expert"), None),
        P(("groups", "expert"), None),
        P("expert", None, "tensor"),
        P("expert", "tensor", None),
    )
    out_specs = P(("groups", "expert", "tensor"), None)
    return jax.shard_map(
        on_device, mesh=mesh, in_specs=in_specs, out_specs=out_specs, check_vma=False
    )
```
